32 devices in a mesh: dp: 16 (over z, y, core), roi: 2 (over x).
Axes of the slice: x: 2, y: 2, z: 4, core: 2. Of those that a mesh axis runs over, the one named last changes fastest.
Arguments:
- feature_maps: bfloat16 [64, 1360, 256], P('dp'), may hold values from -6 to 6
- region_boxes: float32 [9216, 4], P(('dp', 'roi')), may hold values from 0 to 1, as said below
- levels: int32 [9216], P(('dp', 'roi')), may hold values from 0 to 3
- labels: int32 [9216], P(('dp', 'roi')), may hold values from 0 to 80
- image_of_roi: int32 [9216], P(('dp', 'roi')), may hold values from 0 to 63, as said below
- targets: int32 [9216, 4], P(('dp', 'roi')), may hold values from -8192 to 8191
- first_weight: float32 [12544, 1024], P(('dp', 'roi')), may hold values from -0.0546875 to 0.0546875
- second_weight: float32 [1024, 1024], P(('dp', 'roi')), may hold values from -0.1875 to 0.1875
- head_weight: float32 [1024, 85], replicated, may hold values from -0.1875 to 0.1875
- biases: float32 [2133], replicated, may hold values from -1.2 to 1.2
- head_moment: float32 [1024, 85], replicated, as said below
- bias_moment: float32 [2133], replicated, as said below
- left_first: float32 [12544, 12544], P(('dp', 'roi')), as said below
- left_first_root: float32 [12544, 12544], P(('dp', 'roi')), as said below
- right_first: float32 [1024, 1024], P(('dp', 'roi')), as said below
- right_first_root: float32 [1024, 1024], P(('dp', 'roi')), as said below
- left_second: float32 [1024, 1024], P(('dp', 'roi')), as said below
- left_second_root: float32 [1024, 1024], P(('dp', 'roi')), as said below
- right_second: float32 [1024, 1024], P(('dp', 'roi')), as said below
- right_second_root: float32 [1024, 1024], P(('dp', 'roi')), as said below
Outputs:
- region_loss: float32 [9216], P(('dp', 'roi'))
- decoded_boxes: float32 [9216, 4], P(('dp', 'roi'))
- map_gradient: float32 [64, 1360, 256], P('dp', 'roi')
- first_gradient: float32 [12544, 1024], P(('dp', 'roi'))
- new_left_first: float32 [12544, 12544], P(('dp', 'roi'))
- new_right_first: float32 [1024, 1024], P(('dp', 'roi'))
- new_first_weight: float32 [12544, 1024], P(('dp', 'roi'))
- second_gradient: float32 [1024, 1024], P(('dp', 'roi'))
- new_left_second: float32 [1024, 1024], P(('dp', 'roi'))
- new_right_second: float32 [1024, 1024], P(('dp', 'roi'))
- new_second_weight: float32 [1024, 1024], P(('dp', 'roi'))
- head_gradient: float32 [1024, 85], replicated
- new_head_moment: float32 [1024, 85], replicated
- new_head_weight: float32 [1024, 85], replicated
- bias_gradient: float32 [2133], replicated
- new_bias_moment: float32 [2133], replicated
- new_biases: float32 [2133], replicated
The draws below stay inside these ranges and needn't reach their ends.
Inputs may be any that keep to these rules, and one draw needn't show every extreme that they name: `image_of_roi`: every image has exactly 144 regions, and they lie in its group's rows: row r names an image of the group r // 576, that is from that group times 4 up to the next group's first image. `region_boxes`: x1 < x2 and y1 < y2. `left_first`: symmetric. `left_first_root`: symmetric. `right_first`: symmetric. `right_first_root`: symmetric. `left_second`: symmetric. `left_second_root`: symmetric. `right_second`: symmetric. `right_second_root`: symmetric. `head_moment`: positive. `bias_moment`: positive.
All inputs are finite; a program needn't handle non-finite values.
Results may differ from the reference program's by a relative error of at most 0.0055.
The reference program's roundings to bfloat16 on the way count: a program that leaves them out, or rounds other values in their place, can miss the bound.
Values may be sent and summed in bfloat16 or wider, within the bound.
A program may use at most 320 MiB of HBM per device.

```python
import math
import jax
import jax.numpy as jnp
from jax import lax

C = 256
FC = 1024
CLS = 81
POOL = 7
MAP = 32
RPI = 144
IMG_DEV = 4
IMAGES = 64
REGIONS = 9216
CELLS = 1360
FEAT = 12544
OUTS = 85
NB = 2133


def statistic(key, order, diagonal_scale, lowest, highest):
    diagonal_key, noise_key = jax.random.split(key)
    diagonal = diagonal_scale * jnp.exp(jax.random.uniform(diagonal_key, (order,), jnp.float32, math.log(lowest), math.log(highest)))
    noise_matrix = jax.random.normal(noise_key, (order, order), jnp.float32)
    spread = 0.5 * diagonal_scale * math.sqrt(lowest * highest) / math.sqrt(2.0 * order)
    return (noise_matrix + noise_matrix.T) * spread + jnp.diag(diagonal)


def first_scale():
    return 0.02 / math.sqrt(REGIONS)


def second_scale():
    return 0.018 / math.sqrt(REGIONS)


def draw_region_boxes(key, part):
    key = jax.random.fold_in(key, 1)
    center_key, size_key = jax.random.split(key)
    centers = jax.random.uniform(center_key, (REGIONS, 2), jnp.float32, 0.25, 0.75)
    extents = jnp.exp(jax.random.uniform(size_key, (REGIONS, 2), jnp.float32, math.log(0.05), math.log(0.5)))
    return jnp.concatenate([centers - 0.5 * extents, centers + 0.5 * extents], axis=1)


def draw_image_of_roi(key, part):
    key = jax.random.fold_in(key, 2)
    groups = IMAGES // IMG_DEV
    per_group = IMG_DEV * RPI
    group_keys = jax.random.split(key, groups)

    def shuffle_group(group_key):
        return jax.random.permutation(group_key, per_group)
    shuffled = jax.vmap(shuffle_group)(group_keys)
    images = jnp.arange(groups, dtype=jnp.int32)[:, None] * IMG_DEV + shuffled // RPI
    return images.reshape(REGIONS).astype(jnp.int32)


def draw_left_first(key, part):
    key = jax.random.fold_in(key, 3)
    return statistic(key, FEAT, 0.0526 * FC * first_scale() ** 2, 1.0, 4.0)


def draw_left_first_root(key, part):
    key = jax.random.fold_in(key, 4)
    return statistic(key, FEAT, first_scale() ** (-0.5), 0.5, 2.0)


def draw_right_first(key, part):
    key = jax.random.fold_in(key, 5)
    return statistic(key, FC, 0.0526 * FEAT * first_scale() ** 2, 1.0, 4.0)


def draw_right_first_root(key, part):
    key = jax.random.fold_in(key, 6)
    return statistic(key, FC, first_scale() ** (-0.5), 0.5, 2.0)


def draw_left_second(key, part):
    key = jax.random.fold_in(key, 7)
    return statistic(key, FC, 0.0526 * FC * second_scale() ** 2, 1.0, 4.0)


def draw_left_second_root(key, part):
    key = jax.random.fold_in(key, 8)
    return statistic(key, FC, second_scale() ** (-0.5), 0.5, 2.0)


def draw_right_second(key, part):
    key = jax.random.fold_in(key, 9)
    return statistic(key, FC, 0.0526 * FC * second_scale() ** 2, 1.0, 4.0)


def draw_right_second_root(key, part):
    key = jax.random.fold_in(key, 10)
    return statistic(key, FC, second_scale() ** (-0.5), 0.5, 2.0)


def draw_head_moment(key, part):
    key = jax.random.fold_in(key, 11)
    column = jnp.arange(OUTS, dtype=jnp.int32)
    column_scale = jnp.where(column < CLS, 0.045, 0.34) / math.sqrt(REGIONS)
    factor = jnp.exp(jax.random.uniform(key, (FC, OUTS), jnp.float32, 0.0, math.log(4.0)))
    return 0.0101 * (column_scale * column_scale)[None, :] * factor


def draw_bias_moment(key, part):
    key = jax.random.fold_in(key, 12)
    position = jnp.arange(NB, dtype=jnp.int32)
    entry_scale = jnp.where(position < FC, 0.035, jnp.where(position < 2 * FC, 0.045, jnp.where(position < 2 * FC + CLS, 0.11, 0.7))) / math.sqrt(REGIONS)
    factor = jnp.exp(jax.random.uniform(key, (NB,), jnp.float32, 0.0, math.log(4.0)))
    return 0.0101 * entry_scale * entry_scale * factor


def place_ends(values, own_key, smallest, high):
    extent = values.shape
    spot = [jax.random.randint(jax.random.fold_in(own_key, axis), (), 0, extent[axis]) for axis in range(len(extent))]
    values = values.at[tuple(spot)].set(smallest)
    longest = extent.index(max(extent))
    spot[longest] = (spot[longest] + 1) % extent[longest]
    return values.at[tuple(spot)].set(high)


def block_scale(own_key, shape, pieces, smallest, top_value):
    loudness = 1.0
    for axis_at, parts in pieces:
        draws = jax.random.uniform(jax.random.fold_in(jax.random.fold_in(own_key, 6), axis_at), (parts,), jnp.float32, smallest / len(pieces), top_value / len(pieces))
        loudness = loudness * jnp.repeat(jnp.exp(draws), shape[axis_at] // parts).reshape((-1,) + (1,) * (len(shape) - 1 - axis_at))
    return loudness


def scatter_about(stream_key, dims, scale, bound, pieces=(), kind=jnp.bfloat16):
    level = block_scale(stream_key, dims, pieces, -0.22, 0.18) if pieces else 1.0
    values = jax.random.normal(stream_key, dims, jnp.float32) * scale * level
    return jnp.minimum(jnp.maximum(values, -bound), bound).astype(kind)


def setup_inputs(seed: int = 0) -> dict:
    key_of = jax.random.split(jax.random.key(seed), 21)
    feature_maps = scatter_about(key_of[0], (IMAGES, CELLS, C), 1.0, 6.0, ((0, 16),))
    region_boxes = draw_region_boxes(jax.random.fold_in(key_of[20], 71), 0)
    levels = place_ends(jax.random.randint(key_of[2], (REGIONS,), 0, 4), jax.random.fold_in(key_of[2], 1), 0, 3).astype(jnp.int32)
    labels = place_ends(jax.random.randint(key_of[3], (REGIONS,), 0, CLS), jax.random.fold_in(key_of[3], 1), 0, CLS - 1).astype(jnp.int32)
    image_of_roi = draw_image_of_roi(jax.random.fold_in(key_of[20], 71), 0)
    targets = place_ends(jax.random.randint(key_of[5], (REGIONS, 4), -8192, 8192), jax.random.fold_in(key_of[5], 1), -8192, 8191).astype(jnp.int32)
    first_weight = scatter_about(key_of[6], (FEAT, FC), FEAT ** -0.5, 0.0546875, ((0, 32),), jnp.float32)
    second_weight = scatter_about(key_of[7], (FC, FC), FC ** -0.5, 0.1875, ((0, 32),), jnp.float32)
    head_weight = scatter_about(key_of[8], (FC, OUTS), FC ** -0.5, 0.1875, (), jnp.float32)
    biases = scatter_about(key_of[9], (NB,), 0.3, 1.2, (), jnp.float32)
    head_moment = draw_head_moment(jax.random.fold_in(key_of[20], 71), 0)
    bias_moment = draw_bias_moment(jax.random.fold_in(key_of[20], 71), 0)
    left_first = draw_left_first(jax.random.fold_in(key_of[20], 71), 0)
    left_first_root = draw_left_first_root(jax.random.fold_in(key_of[20], 71), 0)
    right_first = draw_right_first(jax.random.fold_in(key_of[20], 71), 0)
    right_first_root = draw_right_first_root(jax.random.fold_in(key_of[20], 71), 0)
    left_second = draw_left_second(jax.random.fold_in(key_of[20], 71), 0)
    left_second_root = draw_left_second_root(jax.random.fold_in(key_of[20], 71), 0)
    right_second = draw_right_second(jax.random.fold_in(key_of[20], 71), 0)
    right_second_root = draw_right_second_root(jax.random.fold_in(key_of[20], 71), 0)
    return dict(feature_maps=feature_maps, region_boxes=region_boxes, levels=levels, labels=labels, image_of_roi=image_of_roi, targets=targets, first_weight=first_weight, second_weight=second_weight, head_weight=head_weight, biases=biases, head_moment=head_moment, bias_moment=bias_moment, left_first=left_first, left_first_root=left_first_root, right_first=right_first, right_first_root=right_first_root, left_second=left_second, left_second_root=left_second_root, right_second=right_second, right_second_root=right_second_root)


BETA = 0.95
DECAY = 0.99
RATE_FIRST = 0.01
RATE_SECOND = 0.03
RATE_HEAD = 0.005
RATE_BIAS = 0.05
EPSILON = 1e-08
FIXED_POINT = 4096.0

@jax.custom_vjp
def low(v):
    return lax.optimization_barrier(v.astype(jnp.bfloat16)).astype(jnp.float32)

@jax.custom_vjp
def low_back(v):
    return v

def low_keep(v):
    return (low(v), None)

def low_pass(kept, grad):
    return (grad,)

def back_keep(v):
    return (v, None)

def back_low(kept, grad):
    return (low(grad),)
low.defvjp(low_keep, low_pass)
low_back.defvjp(back_keep, back_low)

def exact_dot(left_side, right_side):
    return jnp.dot(left_side, right_side, precision=lax.Precision.HIGHEST)

def corner_plan(region_boxes, levels, top_side, pool_size):
    centers = (jnp.arange(pool_size, dtype=jnp.float32) + 0.5) / pool_size
    picked = levels[:, None] == jnp.arange(4, dtype=jnp.int32)[None, :]
    quarter = top_side * top_side
    side_table = jnp.array([top_side, top_side // 2, top_side // 4, top_side // 8], dtype=jnp.int32)
    start_table = jnp.array([0, quarter, quarter + quarter // 4, quarter + quarter // 4 + quarter // 16], dtype=jnp.int32)
    side_cells = lax.optimization_barrier(jnp.sum(jnp.where(picked, side_table[None, :], 0), axis=1)).astype(jnp.int32)
    level_start = lax.optimization_barrier(jnp.sum(jnp.where(picked, start_table[None, :], 0), axis=1)).astype(jnp.int32)
    side_float = side_cells.astype(jnp.float32)[:, None]
    across = region_boxes[:, 0:1] + centers[None, :] * (region_boxes[:, 2:3] - region_boxes[:, 0:1])
    downward = region_boxes[:, 1:2] + centers[None, :] * (region_boxes[:, 3:4] - region_boxes[:, 1:2])
    across = jnp.clip(across * side_float - 0.5, 0.0, side_float - 1.0)
    downward = jnp.clip(downward * side_float - 0.5, 0.0, side_float - 1.0)
    left_col = jnp.floor(across).astype(jnp.int32)
    top_row = jnp.floor(downward).astype(jnp.int32)
    last_cell = side_cells[:, None] - 1
    right_col = jnp.minimum(left_col + 1, last_cell)
    bottom_row = jnp.minimum(top_row + 1, last_cell)
    frac_x = (across - left_col.astype(jnp.float32))[:, None, :]
    frac_y = (downward - top_row.astype(jnp.float32))[:, :, None]
    level_base = level_start[:, None, None]
    width_cells = side_cells[:, None, None]
    corner_cells = [level_base + top_row[:, :, None] * width_cells + left_col[:, None, :], level_base + top_row[:, :, None] * width_cells + right_col[:, None, :], level_base + bottom_row[:, :, None] * width_cells + left_col[:, None, :], level_base + bottom_row[:, :, None] * width_cells + right_col[:, None, :]]
    corner_parts = [(1.0 - frac_y) * (1.0 - frac_x), (1.0 - frac_y) * frac_x, frac_y * (1.0 - frac_x), frac_y * frac_x]
    region_count = region_boxes.shape[0]
    cell_index = jnp.stack(corner_cells, axis=-1).reshape(region_count, pool_size * pool_size, 4).astype(jnp.int32)
    corner_weights = jnp.stack(corner_parts, axis=-1).reshape(region_count, pool_size * pool_size, 4)
    return (cell_index, corner_weights)

def decode_boxes(region_boxes, deltas):
    widths = region_boxes[:, 2] - region_boxes[:, 0]
    heights = region_boxes[:, 3] - region_boxes[:, 1]
    center_x = region_boxes[:, 0] + 0.5 * widths
    center_y = region_boxes[:, 1] + 0.5 * heights
    moved_x = center_x + deltas[:, 0] / 10.0 * widths
    moved_y = center_y + deltas[:, 1] / 10.0 * heights
    new_width = widths * jnp.exp(deltas[:, 2] / 5.0)
    new_height = heights * jnp.exp(deltas[:, 3] / 5.0)
    return jnp.stack([moved_x - 0.5 * new_width, moved_y - 0.5 * new_height, moved_x + 0.5 * new_width, moved_y + 0.5 * new_height], axis=1)

def huber_loss(residue):
    magnitude = jnp.abs(residue)
    return jnp.where(magnitude < 1.0, 0.5 * residue * residue, magnitude - 0.5)

def group_loss(maps_one, boxes_one, level_one, label_one, image_one, target_one, first_low, second_low, head_low, bias_all):
    cell_index, corner_weights = corner_plan(boxes_one, level_one, MAP, POOL)
    flat_rows = image_one[:, None, None] * CELLS + cell_index
    flat_maps = maps_one.reshape(IMG_DEV * CELLS, C)
    pooled = corner_weights[:, :, 0:1] * flat_maps[flat_rows[:, :, 0]]
    for corner in range(1, 4):
        pooled = pooled + corner_weights[:, :, corner:corner + 1] * flat_maps[flat_rows[:, :, corner]]
    pooled_low = low(pooled.reshape(pooled.shape[0], FEAT))
    first_pre = low_back(exact_dot(pooled_low, first_low) + bias_all[:FC])
    first_act = low(jax.nn.silu(first_pre))
    second_pre = low_back(exact_dot(first_act, second_low) + bias_all[FC:2 * FC])
    second_act = low(jax.nn.silu(second_pre))
    head_out = low_back(exact_dot(second_act, head_low) + bias_all[2 * FC:])
    logits = head_out[:, :CLS]
    deltas = head_out[:, CLS:]
    largest = lax.optimization_barrier(jnp.max(logits, axis=1, keepdims=True))
    log_total = largest[:, 0] + jnp.log(lax.optimization_barrier(jnp.sum(jnp.exp(logits - largest), axis=1)))
    label_hot = label_one[:, None] == jnp.arange(CLS, dtype=jnp.int32)[None, :]
    chosen = lax.optimization_barrier(jnp.sum(jnp.where(label_hot, logits, 0.0), axis=1))
    foreground = (label_one > 0).astype(jnp.float32)
    residue = deltas - target_one.astype(jnp.float32) / FIXED_POINT
    losses = log_total - chosen + foreground * lax.optimization_barrier(jnp.sum(huber_loss(residue), axis=1))
    return (losses, deltas)

def shampoo_step(gradient, weight, left_stat, left_root, right_stat, right_root, step_rate):
    rounded = low(gradient)
    new_left = BETA * left_stat + (1.0 - BETA) * exact_dot(rounded, rounded.T)
    new_right = BETA * right_stat + (1.0 - BETA) * exact_dot(rounded.T, rounded)
    update = exact_dot(exact_dot(low(left_root), rounded), right_root)
    return (new_left, new_right, weight - step_rate * update)

def diagonal_step(gradient, weight, moment, step_rate):
    new_moment = DECAY * moment + (1.0 - DECAY) * gradient * gradient
    return (new_moment, weight - step_rate * gradient / (jnp.sqrt(new_moment) + EPSILON))

def reference(feature_maps, region_boxes, levels, labels, image_of_roi, targets, first_weight, second_weight, head_weight, biases, head_moment, bias_moment, left_first, left_first_root, right_first, right_first_root, left_second, left_second_root, right_second, right_second_root):
    groups = IMAGES // IMG_DEV
    per_group = IMG_DEV * RPI
    maps_grouped = feature_maps.astype(jnp.float32).reshape(groups, IMG_DEV, CELLS, C)
    group_index = jnp.arange(groups, dtype=jnp.int32)
    group_items = (region_boxes.reshape(groups, per_group, 4), levels.reshape(groups, per_group), labels.reshape(groups, per_group), (image_of_roi.reshape(groups, per_group) - group_index[:, None] * IMG_DEV).astype(jnp.int32), targets.reshape(groups, per_group, 4))

    def total_loss(maps_all, first_param, second_param, head_param, bias_param):
        first_low = low(first_param)
        second_low = low(second_param)
        head_low = low(head_param)

        def one_group(running_sum, slices):
            maps_one, boxes_one, level_one, label_one, image_one, target_one = slices
            losses, deltas = group_loss(maps_one, boxes_one, level_one, label_one, image_one, target_one, first_low, second_low, head_low, bias_param)
            return (running_sum + jnp.sum(losses), (losses, deltas))
        loss_sum, (losses, deltas) = lax.scan(jax.checkpoint(one_group), jnp.zeros((), jnp.float32), (maps_all,) + group_items)
        return (loss_sum / REGIONS, (losses.reshape(REGIONS), deltas.reshape(REGIONS, 4)))
    mean_loss, pullback, extras = jax.vjp(total_loss, maps_grouped, first_weight, second_weight, head_weight, biases, has_aux=True)
    region_loss, deltas = extras
    map_grads, first_gradient, second_gradient, head_gradient, bias_gradient = pullback(jnp.ones_like(mean_loss))
    map_gradient = map_grads.reshape(IMAGES, CELLS, C)
    decoded = decode_boxes(region_boxes, deltas)
    new_left_first, new_right_first, new_first_weight = shampoo_step(first_gradient, first_weight, left_first, left_first_root, right_first, right_first_root, RATE_FIRST)
    new_left_second, new_right_second, new_second_weight = shampoo_step(second_gradient, second_weight, left_second, left_second_root, right_second, right_second_root, RATE_SECOND)
    new_head_moment, new_head_weight = diagonal_step(head_gradient, head_weight, head_moment, RATE_HEAD)
    new_bias_moment, new_biases = diagonal_step(bias_gradient, biases, bias_moment, RATE_BIAS)
    return (region_loss, decoded, map_gradient, first_gradient, new_left_first, new_right_first, new_first_weight, second_gradient, new_left_second, new_right_second, new_second_weight, head_gradient, new_head_moment, new_head_weight, bias_gradient, new_bias_moment, new_biases)
```

```python
import functools

import jax
import jax.numpy as jnp
from jax import lax
from jax.experimental import pallas as pl
from jax.experimental.pallas import tpu as pltpu
from jax.sharding import PartitionSpec as P

POOL = 7
BINS = POOL * POOL
MAP = 32
TILE = 16
FINE = MAP * MAP
COLS = 896
MIB = 1 << 20

BETA = 0.95
DECAY = 0.99
RATE_FIRST = 0.01
RATE_SECOND = 0.03
RATE_HEAD = 0.005
RATE_BIAS = 0.05
EPSILON = 1e-08
FIXED_POINT = 4096.0


def round_up(value, unit):
    return (value + unit - 1) // unit * unit


def sample_points(boxes, levels):
    centers = (jnp.arange(POOL, dtype=jnp.float32) + 0.5) / POOL
    side = (MAP >> levels).astype(jnp.float32)[:, None]
    across = boxes[:, 0:1] + centers[None, :] * (boxes[:, 2:3] - boxes[:, 0:1])
    downward = boxes[:, 1:2] + centers[None, :] * (boxes[:, 3:4] - boxes[:, 1:2])
    across = jnp.clip(across * side - 0.5, 0.0, side - 1.0)
    downward = jnp.clip(downward * side - 0.5, 0.0, side - 1.0)
    return across, downward


def decode_boxes(region_boxes, deltas):
    widths = region_boxes[:, 2] - region_boxes[:, 0]
    heights = region_boxes[:, 3] - region_boxes[:, 1]
    center_x = region_boxes[:, 0] + 0.5 * widths
    center_y = region_boxes[:, 1] + 0.5 * heights
    moved_x = center_x + deltas[:, 0] / 10.0 * widths
    moved_y = center_y + deltas[:, 1] / 10.0 * heights
    new_width = widths * jnp.exp(deltas[:, 2] / 5.0)
    new_height = heights * jnp.exp(deltas[:, 3] / 5.0)
    return jnp.stack(
        [
            moved_x - 0.5 * new_width,
            moved_y - 0.5 * new_height,
            moved_x + 0.5 * new_width,
            moved_y + 0.5 * new_height,
        ],
        axis=1,
    )


def huber_loss(residue):
    magnitude = jnp.abs(residue)
    return jnp.where(magnitude < 1.0, 0.5 * residue * residue, magnitude - 0.5)


def silu_slope(values):
    sigmoid = jax.nn.sigmoid(values)
    return sigmoid * (1.0 + values * (1.0 - sigmoid))


def rows_by_rows(left_side, right_side):
    return lax.dot_general(
        left_side, right_side, (((1,), (1,)), ((), ())), preferred_element_type=jnp.float32
    )


def cols_by_cols(left_side, right_side):
    return lax.dot_general(
        left_side, right_side, (((0,), (0,)), ((), ())), preferred_element_type=jnp.float32
    )


def hat(distance):
    return jnp.maximum(1.0 - jnp.abs(distance), 0.0)


def in_order(from_shift):
    members = len(from_shift)
    me = lax.axis_index("roi")
    if members == 2:
        first = jnp.where(me == 0, from_shift[0], from_shift[1])
        second = jnp.where(me == 0, from_shift[1], from_shift[0])
        return jnp.stack([first, second])
    doubled = jnp.stack(from_shift + from_shift)
    return lax.dynamic_slice_in_dim(doubled, lax.rem(members - me, members), members, 0)


def gather_members(block):
    members = lax.axis_size("roi")
    got = [block]
    for shift in range(1, members):
        got.append(lax.ppermute(block, "roi", [((i + shift) % members, i) for i in range(members)]))
    return in_order(got)


def trade_members(parts):
    members = lax.axis_size("roi")
    me = lax.axis_index("roi")
    got = [lax.dynamic_index_in_dim(parts, me, 0, keepdims=False)]
    for shift in range(1, members):
        target = lax.rem(me + members - shift, members)
        part = lax.dynamic_index_in_dim(parts, target, 0, keepdims=False)
        got.append(lax.ppermute(part, "roi", [((i + shift) % members, i) for i in range(members)]))
    return in_order(got)


def lane_coordinates(rows, first_lane, lanes):
    cell = lax.broadcasted_iota(jnp.int32, (rows, lanes), 1) + first_lane
    return cell_coordinates(cell)


def cell_coordinates(cell):
    second = cell - FINE
    third = second - FINE // 4
    fourth = third - FINE // 16
    rest = cell - (FINE + FINE // 4 + FINE // 16 + FINE // 64)
    row = jnp.where(
        second < 0,
        cell >> 5,
        jnp.where(
            third < 0,
            second >> 4,
            jnp.where(fourth < 0, (third >> 3) + 32, (fourth >> 2) + 64),
        ),
    )
    column = jnp.where(
        second < 0,
        cell & 31,
        jnp.where(third < 0, second & 15, jnp.where(fourth < 0, third & 7, fourth & 3)),
    )
    row = jnp.where(rest < 0, row, 1000)
    return row.astype(jnp.float32), column.astype(jnp.float32)


def pool_kernel(fine_ref, coarse_ref, place_ref, maps_ref, out_ref, high, low, total):
    tile = pl.program_id(0)
    cells = maps_ref.shape[1]

    def part(first, count, column_of_row, start):
        chunk = 256 if count % 256 == 0 else 128
        for at in range(0, count, chunk):
            row_of, column_of = lane_coordinates(TILE, first + at, chunk)
            across = [hat(place_ref[:, j : j + 1] - column_of) for j in range(POOL)]
            for i in range(POOL):
                spot = column_of_row + i
                down = hat(place_ref[:, spot : spot + 1] - row_of)
                for j in range(POOL):
                    weight = down * across[j]
                    big = weight.astype(jnp.bfloat16)
                    rows = pl.ds((i * POOL + j) * TILE, TILE)
                    high[rows, pl.ds(at, chunk)] = big
                    low[rows, pl.ds(at, chunk)] = (weight - big.astype(jnp.float32)).astype(
                        jnp.bfloat16
                    )
        maps = maps_ref[0, pl.ds(first, count), :]
        product = jnp.dot(high[:, :count], maps, preferred_element_type=jnp.float32)
        product += jnp.dot(low[:, :count], maps, preferred_element_type=jnp.float32)
        if start:
            total[...] = product
        else:
            total[...] += product

    has_fine = fine_ref[tile] > 0
    has_coarse = coarse_ref[tile] > 0

    @pl.when(has_fine)
    def _():
        part(0, FINE, POOL, True)

    @pl.when(jnp.logical_not(has_fine))
    def _():
        total[...] = jnp.zeros_like(total)

    @pl.when(has_coarse)
    def _():
        part(FINE, cells - FINE, 2 * POOL, False)

    channels = maps_ref.shape[2]
    for b in range(BINS):
        out_ref[:, b * channels : (b + 1) * channels] = total[
            b * TILE : (b + 1) * TILE, :
        ].astype(jnp.bfloat16)


def pool(fine, coarse, places, maps, per_image):
    regions = places.shape[0]
    cells, channels = maps.shape[1:]
    tiles = per_image // TILE
    return pl.pallas_call(
        pool_kernel,
        grid_spec=pltpu.PrefetchScalarGridSpec(
            num_scalar_prefetch=2,
            grid=(regions // TILE,),
            in_specs=[
                pl.BlockSpec((TILE, 128), lambda t, *_: (t, 0)),
                pl.BlockSpec((1, cells, channels), lambda t, *_: (t // tiles, 0, 0)),
            ],
            out_specs=pl.BlockSpec((TILE, BINS * channels), lambda t, *_: (t, 0)),
            scratch_shapes=[
                pltpu.VMEM((BINS * TILE, FINE), jnp.bfloat16),
                pltpu.VMEM((BINS * TILE, FINE), jnp.bfloat16),
                pltpu.VMEM((BINS * TILE, channels), jnp.float32),
            ],
        ),
        out_shape=jax.ShapeDtypeStruct((regions, BINS * channels), jnp.bfloat16),
        compiler_params=pltpu.CompilerParams(vmem_limit_bytes=40 * MIB),
        cost_estimate=pl.CostEstimate(
            flops=4 * regions * BINS * 512 * channels,
            bytes_accessed=2 * regions * BINS * channels,
            transcendentals=0,
        ),
        name="pool",
    )(fine, coarse, places, maps)


def unpool_kernel(fine_ref, coarse_ref, place_ref, grad_ref, out_ref, weight, grads, *, tiles):
    tile = pl.program_id(0)
    cells, channels = out_ref.shape[1:]
    lanes = weight.shape[1]

    @pl.when(tile == 0)
    def _():
        grads[BINS * TILE :, :] = jnp.zeros_like(grads[BINS * TILE :, :])

    @pl.when(lax.rem(tile, tiles) == 0)
    def _():
        out_ref[...] = jnp.zeros_like(out_ref)

    for b in range(BINS):
        grads[b * TILE : (b + 1) * TILE, :] = grad_ref[:, b * channels : (b + 1) * channels]
    across = place_ref[0, 0:1, :]

    @pl.when(fine_ref[tile] > 0)
    def _():
        down = place_ref[0, 1:2, :]
        column = lax.broadcasted_iota(jnp.int32, (MAP, lanes), 0).astype(jnp.float32)
        over = hat(across - column)
        for y in range(MAP):
            weight[y * MAP : (y + 1) * MAP, :] = (hat(down - float(y)) * over).astype(jnp.bfloat16)
        out_ref[0, :FINE, :] += jnp.dot(
            weight[:FINE, :], grads[...], preferred_element_type=jnp.float32
        )

    @pl.when(coarse_ref[tile] > 0)
    def _():
        down = place_ref[0, 2:3, :]
        for at in range(FINE, cells, 16):
            cell = lax.broadcasted_iota(jnp.int32, (16, lanes), 0) + at
            row_of, column_of = cell_coordinates(cell)
            weight[at - FINE : at - FINE + 16, :] = (
                hat(down - row_of) * hat(across - column_of)
            ).astype(jnp.bfloat16)
        out_ref[0, FINE:, :] += jnp.dot(
            weight[: cells - FINE, :], grads[...], preferred_element_type=jnp.float32
        )


def unpool(fine, coarse, lane_places, grads, images, cells, channels):
    regions = grads.shape[0]
    count = regions // TILE
    tiles = count // images
    lanes = lane_places.shape[2]
    return pl.pallas_call(
        functools.partial(unpool_kernel, tiles=tiles),
        grid_spec=pltpu.PrefetchScalarGridSpec(
            num_scalar_prefetch=2,
            grid=(count,),
            in_specs=[
                pl.BlockSpec((1, 8, lanes), lambda t, *_: (t, 0, 0)),
                pl.BlockSpec((TILE, BINS * channels), lambda t, *_: (t, 0)),
            ],
            out_specs=pl.BlockSpec((1, cells, channels), lambda t, *_: (t // tiles, 0, 0)),
            scratch_shapes=[
                pltpu.VMEM((FINE, lanes), jnp.bfloat16),
                pltpu.VMEM((lanes, channels), jnp.bfloat16),
            ],
        ),
        out_shape=jax.ShapeDtypeStruct((images, cells, channels), jnp.float32),
        compiler_params=pltpu.CompilerParams(vmem_limit_bytes=40 * MIB),
        cost_estimate=pl.CostEstimate(
            flops=2 * regions * BINS * 512 * channels,
            bytes_accessed=2 * regions * BINS * channels,
            transcendentals=0,
        ),
        name="unpool",
    )(fine, coarse, lane_places, grads)


def shampoo_kernel(left_ref, root_ref, full_ref, own_ref, right_root_ref, weight_ref,
                   new_left_ref, new_weight_ref, mixed, *, rate):
    step = pl.program_id(0)
    members, _, width = full_ref.shape

    @pl.when(step == 0)
    def _():
        mixed[...] = jnp.zeros_like(mixed)

    root = root_ref[...].astype(jnp.bfloat16)
    gram = rows_by_rows(own_ref[0], full_ref[0])
    for member in range(1, members):
        gram += rows_by_rows(own_ref[member], full_ref[member])
    new_left_ref[...] = BETA * left_ref[...] + (1.0 - BETA) * gram
    for member in range(members):
        mixed[:, member * width : (member + 1) * width] += jnp.dot(
            root, full_ref[member], preferred_element_type=jnp.float32
        )

    @pl.when(step == pl.num_programs(0) - 1)
    def _():
        value = mixed[...]
        high = value.astype(jnp.bfloat16)
        low = (value - high.astype(jnp.float32)).astype(jnp.bfloat16)
        update = jnp.dot(high, right_root_ref[...], preferred_element_type=jnp.float32)
        update += jnp.dot(low, right_root_ref[...], preferred_element_type=jnp.float32)
        new_weight_ref[...] = weight_ref[...] - rate * update


def shampoo(left, root, full, own, right_root, weight, rate):
    rows, order = left.shape
    members, _, width = full.shape
    hidden = members * width
    return pl.pallas_call(
        functools.partial(shampoo_kernel, rate=rate),
        grid=(order // COLS,),
        in_specs=[
            pl.BlockSpec((rows, COLS), lambda t: (0, t)),
            pl.BlockSpec((rows, COLS), lambda t: (0, t)),
            pl.BlockSpec((members, COLS, width), lambda t: (0, t, 0)),
            pl.BlockSpec((members, rows, width), lambda t: (0, 0, 0)),
            pl.BlockSpec((hidden, hidden), lambda t: (0, 0)),
            pl.BlockSpec((rows, hidden), lambda t: (0, 0)),
        ],
        out_specs=[
            pl.BlockSpec((rows, COLS), lambda t: (0, t)),
            pl.BlockSpec((rows, hidden), lambda t: (0, 0)),
        ],
        out_shape=[
            jax.ShapeDtypeStruct((rows, order), jnp.float32),
            jax.ShapeDtypeStruct((rows, hidden), jnp.float32),
        ],
        scratch_shapes=[pltpu.VMEM((rows, hidden), jnp.float32)],
        compiler_params=pltpu.CompilerParams(vmem_limit_bytes=48 * MIB),
        cost_estimate=pl.CostEstimate(
            flops=4 * rows * order * hidden,
            bytes_accessed=12 * rows * order + 2 * order * hidden,
            transcendentals=0,
        ),
        name="shampoo",
    )(left, root, full, own, right_root, weight)


def diagonal_step(gradient, weight, moment, step_rate):
    new_moment = DECAY * moment + (1.0 - DECAY) * gradient * gradient
    return (new_moment, weight - step_rate * gradient / (jnp.sqrt(new_moment) + EPSILON))


def local(
    feature_maps,
    region_boxes,
    levels,
    labels,
    image_of_roi,
    targets,
    first_weight,
    second_weight,
    head_weight,
    biases,
    head_moment,
    bias_moment,
    left_first,
    left_first_root,
    right_first,
    right_first_root,
    left_second,
    left_second_root,
    right_second,
    right_second_root,
):
    groups = lax.axis_size("dp")
    members = lax.axis_size("roi")
    dp = lax.axis_index("dp")
    me = lax.axis_index("roi")
    owner = dp * members + me
    region_count = region_boxes.shape[0]
    group_regions = region_count * members
    images, cells, channels = feature_maps.shape
    per_image = group_regions // images
    owned, hidden = first_weight.shape
    width = hidden // members
    owned_second = second_weight.shape[0]
    features = owned * members * groups
    classes = head_weight.shape[1] - 4
    outs = classes + 4
    loss_scale = 1.0 / (region_count * groups * members)

    first_low = first_weight.astype(jnp.bfloat16)
    column_parts = jnp.swapaxes(first_low.reshape(owned, members, width), 0, 1)
    second_block = second_weight.astype(jnp.bfloat16).reshape(owned_second * members, width)
    parts = jnp.concatenate(
        [column_parts, jnp.broadcast_to(second_block, (members,) + second_block.shape)], axis=1
    )
    traded = trade_members(parts)
    payload = jnp.concatenate(
        [
            traded[:, :owned].reshape(members * owned, width),
            traded[:, owned:].reshape(members * members * owned_second, width),
        ],
        axis=0,
    )
    gathered = lax.all_gather(payload, "dp", axis=0)
    first_half = gathered[:, : members * owned].reshape(features, width)
    second_full = gathered[:, members * owned :].reshape(hidden, hidden)

    info = jnp.concatenate(
        [
            region_boxes,
            jnp.stack([levels, image_of_roi - dp * images, labels], axis=1).astype(jnp.float32),
            targets.astype(jnp.float32),
        ],
        axis=1,
    )
    info = gather_members(info).reshape(group_regions, info.shape[1])
    key = info[:, 5] * 4.0 + info[:, 4]
    number = jnp.arange(group_regions, dtype=jnp.int32)
    ahead = (key[None, :] < key[:, None]) | (
        (key[None, :] == key[:, None]) & (number[None, :] < number[:, None])
    )
    position = jnp.sum(ahead.astype(jnp.int32), axis=1)
    chosen = (position[None, :] == number[:, None]).astype(jnp.float32)
    info = jnp.dot(chosen, info, precision=lax.Precision.HIGHEST)
    boxes = info[:, :4]
    level = jnp.round(info[:, 4]).astype(jnp.int32)
    across, down = sample_points(boxes, level)
    fine_down = jnp.where(level[:, None] == 0, down, -64.0)
    coarse_down = jnp.where(
        level[:, None] == 0, -64.0, down + 32.0 * (level[:, None] - 1).astype(jnp.float32)
    )
    count = group_regions // TILE
    fine = jnp.max((level == 0).astype(jnp.int32).reshape(count, TILE), axis=1)
    coarse = jnp.max((level > 0).astype(jnp.int32).reshape(count, TILE), axis=1)
    places = jnp.pad(
        jnp.concatenate([across, fine_down, coarse_down], axis=1), ((0, 0), (0, 128 - 3 * POOL))
    )
    by_tile = places[:, : 3 * POOL].reshape(count, TILE, 3, POOL)
    by_tile = jnp.transpose(by_tile, (0, 2, 3, 1))
    lane_shape = (count, POOL, POOL, TILE)
    lanes = round_up(BINS * TILE, 128)
    lane_places = jnp.stack(
        [
            jnp.broadcast_to(by_tile[:, 0, None, :, :], lane_shape),
            jnp.broadcast_to(by_tile[:, 1, :, None, :], lane_shape),
            jnp.broadcast_to(by_tile[:, 2, :, None, :], lane_shape),
        ],
        axis=1,
    ).reshape(count, 3, BINS * TILE)
    lane_places = jnp.pad(lane_places, ((0, 0), (0, 5), (0, lanes - BINS * TILE)))

    padded_maps = jnp.pad(feature_maps, ((0, 0), (0, round_up(cells, 128) - cells), (0, 0)))
    pooled = pool(fine, coarse, places, padded_maps, per_image)

    head_low = head_weight.astype(jnp.bfloat16)
    bias_first = lax.dynamic_slice_in_dim(biases, me * width, width)
    bias_second = biases[hidden : 2 * hidden]
    bias_head = biases[2 * hidden :]
    first_pre = jnp.dot(pooled, first_half, preferred_element_type=jnp.float32) + bias_first
    first_act = jax.nn.silu(first_pre).astype(jnp.bfloat16)
    act_rows = trade_members(first_act.reshape(members, region_count, width))
    act_rows = jnp.swapaxes(act_rows, 0, 1).reshape(region_count, hidden)
    second_pre = jnp.dot(act_rows, second_full, preferred_element_type=jnp.float32) + bias_second
    second_act = jax.nn.silu(second_pre).astype(jnp.bfloat16)
    head_out = jnp.dot(second_act, head_low, preferred_element_type=jnp.float32) + bias_head
    own_info = lax.dynamic_slice_in_dim(info, me * region_count, region_count, 0)
    own_labels = jnp.round(own_info[:, 6]).astype(jnp.int32)
    logits = head_out[:, :classes]
    deltas = head_out[:, classes:]
    largest = jnp.max(logits, axis=1, keepdims=True)
    shifted = jnp.exp(logits - largest)
    exp_total = jnp.sum(shifted, axis=1, keepdims=True)
    log_total = largest[:, 0] + jnp.log(exp_total[:, 0])
    label_hot = own_labels[:, None] == jnp.arange(classes, dtype=jnp.int32)[None, :]
    picked = jnp.sum(jnp.where(label_hot, logits, 0.0), axis=1)
    foreground = (own_labels > 0).astype(jnp.float32)
    residue = deltas - own_info[:, 7:11] / FIXED_POINT
    loss = log_total - picked + foreground * jnp.sum(huber_loss(residue), axis=1)
    decoded = decode_boxes(own_info[:, :4], deltas)
    results = gather_members(jnp.concatenate([loss[:, None], decoded], axis=1))
    results = results.reshape(group_regions, 5)
    own_position = lax.dynamic_slice_in_dim(position, me * region_count, region_count)
    own_chosen = (own_position[:, None] == number[None, :]).astype(jnp.float32)
    results = jnp.dot(own_chosen, results, precision=lax.Precision.HIGHEST)

    grad_logits = (shifted / exp_total - label_hot.astype(jnp.float32)) * loss_scale
    grad_deltas = foreground[:, None] * jnp.clip(residue, -1.0, 1.0) * loss_scale
    grad_out = jnp.concatenate([grad_logits, grad_deltas], axis=1).astype(jnp.bfloat16)
    head_term = cols_by_cols(second_act, grad_out)
    grad_second_act = rows_by_rows(grad_out, head_low)
    grad_second = (grad_second_act * silu_slope(second_pre)).astype(jnp.bfloat16)
    group_second = gather_members(grad_second).reshape(group_regions, hidden)
    second_rows = lax.dynamic_slice_in_dim(second_full, me * width, width, 0)
    grad_first = (rows_by_rows(group_second, second_rows) * silu_slope(first_pre)).astype(
        jnp.bfloat16
    )
    first_term = cols_by_cols(pooled, grad_first)
    second_term = cols_by_cols(first_act, group_second)
    first_sum = lax.psum_scatter(first_term, "dp", scatter_dimension=0, tiled=True)
    second_sum = lax.psum_scatter(second_term, "dp", scatter_dimension=0, tiled=True)

    grad_pooled = rows_by_rows(grad_first, first_half).astype(jnp.bfloat16)
    map_partial = unpool(fine, coarse, lane_places, grad_pooled, images, cells, channels)
    map_parts = map_partial.reshape(images, members, cells // members, channels)
    map_parts = jnp.swapaxes(map_parts, 0, 1)
    map_own = lax.dynamic_index_in_dim(map_parts, me, 0, keepdims=False)
    map_traded = trade_members(map_parts.astype(jnp.bfloat16)).astype(jnp.float32)
    keep = (jnp.arange(members) == me)[:, None, None, None]
    map_gradient = map_own + jnp.sum(jnp.where(keep, 0.0, map_traded), axis=0)

    zeros = jnp.zeros((hidden,), jnp.float32)
    bias_term = jnp.concatenate(
        [
            lax.dynamic_update_slice_in_dim(
                zeros, jnp.sum(grad_first, axis=0, dtype=jnp.float32), me * width, 0
            ),
            jnp.sum(grad_second, axis=0, dtype=jnp.float32),
            jnp.sum(grad_out, axis=0, dtype=jnp.float32),
        ]
    )
    head_gradient, bias_gradient = lax.psum((head_term, bias_term), ("dp", "roi"))

    first_gradient = trade_members(first_sum.reshape(members, owned, width))
    first_gradient = jnp.swapaxes(first_gradient, 0, 1).reshape(owned, hidden)
    devices = groups * members
    second_gradient = lax.ppermute(
        second_sum,
        ("dp", "roi"),
        [((b % groups) * members + b // groups, b) for b in range(devices)],
    )
    first_reduced = lax.all_gather(first_sum.astype(jnp.bfloat16), ("roi", "dp"), axis=0)
    first_reduced = first_reduced.reshape(members, features, width)
    second_reduced = lax.all_gather(
        second_sum.astype(jnp.bfloat16), ("roi", "dp"), axis=0, tiled=True
    )
    right_roots = jnp.stack([right_first_root, right_second_root]).astype(jnp.bfloat16)
    right_roots = lax.all_gather(right_roots, ("dp", "roi"), axis=1, tiled=True)

    own_first = lax.dynamic_slice_in_dim(first_reduced, owner * owned, owned, 1)
    new_left_first, new_first_weight = shampoo(
        left_first, left_first_root, first_reduced, own_first, right_roots[0], first_weight,
        RATE_FIRST,
    )
    own_rows = right_first.shape[0]
    which = owner * own_rows // width
    own_columns = lax.dynamic_slice(
        first_reduced, (which, 0, owner * own_rows - which * width), (1, features, own_rows)
    )[0]
    first_gram = jnp.concatenate(
        [cols_by_cols(own_columns, first_reduced[member]) for member in range(members)], axis=1
    )
    new_right_first = BETA * right_first + (1.0 - BETA) * first_gram

    own_second = lax.dynamic_slice_in_dim(second_reduced, owner * owned_second, owned_second, 0)
    own_columns = lax.dynamic_slice_in_dim(second_reduced, owner * own_rows, own_rows, 1)
    new_left_second = BETA * left_second + (1.0 - BETA) * rows_by_rows(own_second, second_reduced)
    new_right_second = BETA * right_second + (1.0 - BETA) * cols_by_cols(
        own_columns, second_reduced
    )
    mixed = jnp.dot(
        left_second_root.astype(jnp.bfloat16), second_reduced, preferred_element_type=jnp.float32
    )
    mixed_high = mixed.astype(jnp.bfloat16)
    mixed_low = (mixed - mixed_high.astype(jnp.float32)).astype(jnp.bfloat16)
    update = jnp.dot(mixed_high, right_roots[1], preferred_element_type=jnp.float32) + jnp.dot(
        mixed_low, right_roots[1], preferred_element_type=jnp.float32
    )
    new_second_weight = second_weight - RATE_SECOND * update

    new_head_moment, new_head_weight = diagonal_step(
        head_gradient, head_weight, head_moment, RATE_HEAD
    )
    new_bias_moment, new_biases = diagonal_step(bias_gradient, biases, bias_moment, RATE_BIAS)
    return (
        results[:, 0],
        results[:, 1:],
        map_gradient,
        first_gradient,
        new_left_first,
        new_right_first,
        new_first_weight,
        second_gradient,
        new_left_second,
        new_right_second,
        new_second_weight,
        head_gradient,
        new_head_moment,
        new_head_weight,
        bias_gradient,
        new_bias_moment,
        new_biases,
    )


def solution(mesh):
    rows = P(("dp", "roi"), None)
    flat = P(("dp", "roi"))
    return jax.shard_map(
        local,
        mesh=mesh,
        in_specs=(P("dp", None, None), rows, flat, flat, flat, rows, rows, rows)
        + (P(),) * 4
        + (rows,) * 8,
        out_specs=(flat, rows, P("dp", "roi", None)) + (rows,) * 8 + (P(),) * 6,
        check_vma=False,
    )
```

```python
import functools
import math

import jax
import jax.numpy as jnp
from jax import lax
from jax.experimental import pallas as pl
from jax.experimental.pallas import tpu as pltpu
from jax.sharding import PartitionSpec as P

POOL = 7
BINS = POOL * POOL
MAP = 32
TILE = 16
FINE = MAP * MAP
COLS = 896
MIB = 1 << 20

BETA = 0.95
DECAY = 0.99
RATE_FIRST = 0.01
RATE_SECOND = 0.03
RATE_HEAD = 0.005
RATE_BIAS = 0.05
EPSILON = 1e-08
FIXED_POINT = 4096.0


def round_up(value, unit):
    return (value + unit - 1) // unit * unit


def sample_points(boxes, levels):
    centers = (jnp.arange(POOL, dtype=jnp.float32) + 0.5) / POOL
    side = (MAP >> levels).astype(jnp.float32)[:, None]
    across = boxes[:, 0:1] + centers[None, :] * (boxes[:, 2:3] - boxes[:, 0:1])
    downward = boxes[:, 1:2] + centers[None, :] * (boxes[:, 3:4] - boxes[:, 1:2])
    across = jnp.clip(across * side - 0.5, 0.0, side - 1.0)
    downward = jnp.clip(downward * side - 0.5, 0.0, side - 1.0)
    return across, downward


def decode_boxes(region_boxes, deltas):
    widths = region_boxes[:, 2] - region_boxes[:, 0]
    heights = region_boxes[:, 3] - region_boxes[:, 1]
    center_x = region_boxes[:, 0] + 0.5 * widths
    center_y = region_boxes[:, 1] + 0.5 * heights
    moved_x = center_x + deltas[:, 0] / 10.0 * widths
    moved_y = center_y + deltas[:, 1] / 10.0 * heights
    new_width = widths * jnp.exp(deltas[:, 2] / 5.0)
    new_height = heights * jnp.exp(deltas[:, 3] / 5.0)
    return jnp.stack(
        [
            moved_x - 0.5 * new_width,
            moved_y - 0.5 * new_height,
            moved_x + 0.5 * new_width,
            moved_y + 0.5 * new_height,
        ],
        axis=1,
    )


def huber_loss(residue):
    magnitude = jnp.abs(residue)
    return jnp.where(magnitude < 1.0, 0.5 * residue * residue, magnitude - 0.5)


def silu_slope(values):
    sigmoid = jax.nn.sigmoid(values)
    return sigmoid * (1.0 + values * (1.0 - sigmoid))


def rows_by_rows(left_side, right_side):
    return lax.dot_general(
        left_side, right_side, (((1,), (1,)), ((), ())), preferred_element_type=jnp.float32
    )


def cols_by_cols(left_side, right_side):
    return lax.dot_general(
        left_side, right_side, (((0,), (0,)), ((), ())), preferred_element_type=jnp.float32
    )


def hat(distance):
    return jnp.maximum(1.0 - jnp.abs(distance), 0.0)


def in_order(from_shift):
    members = len(from_shift)
    me = lax.axis_index("roi")
    if members == 2:
        first = jnp.where(me == 0, from_shift[0], from_shift[1])
        second = jnp.where(me == 0, from_shift[1], from_shift[0])
        return jnp.stack([first, second])
    doubled = jnp.stack(from_shift + from_shift)
    return lax.dynamic_slice_in_dim(doubled, lax.rem(members - me, members), members, 0)


def gather_members(block):
    members = lax.axis_size("roi")
    got = [block]
    for shift in range(1, members):
        got.append(lax.ppermute(block, "roi", [((i + shift) % members, i) for i in range(members)]))
    return in_order(got)


def trade_members(parts):
    members = lax.axis_size("roi")
    me = lax.axis_index("roi")
    got = [lax.dynamic_index_in_dim(parts, me, 0, keepdims=False)]
    for shift in range(1, members):
        target = lax.rem(me + members - shift, members)
        part = lax.dynamic_index_in_dim(parts, target, 0, keepdims=False)
        got.append(lax.ppermute(part, "roi", [((i + shift) % members, i) for i in range(members)]))
    return in_order(got)


def flip(index, bits):
    value, bit = index, 1
    while bit <= bits:
        if bits & bit:
            value = value + bit * (1 - 2 * (index // bit % 2))
        bit *= 2
    return value


def piece_rows(rows):
    return max(n for n in range(16, 257, 16) if rows % n == 0)


def lowest_bit(value):
    return (value & -value).bit_length() - 1


SPLIT = (0, 0, 2, 2, 2)
ORDERS = (
    (1, 2, 0, 3, 4),
    (1, 2, 0, 3, 4),
    (1, 2, 3, 0, 4),
    (1, 3, 2, 0, 4),
    (0, 1, 2, 3, 4),
    (3, 0, 1, 2, 4),
    (3, 1, 2, 0, 4),
)


class SumPlan:
    def __init__(self, groups):
        self.groups = groups
        self.stages = groups.bit_length() - 1
        even = range(groups - 2, -1, -2)
        self.order = [r for r in even if r % 4 == 2] + [r for r in even if r % 4 == 0]

    def count(self, stage):
        return self.groups >> (stage + 1)

    def slot(self, stage, r):
        return r >> (stage + 1)


def sum_kernel(plan, arrays, *refs):
    inputs = refs[:arrays]
    outputs = refs[arrays : 3 * arrays]
    rest = refs[3 * arrays :]
    groups, stages = plan.groups, plan.stages
    me = lax.axis_index("dp")
    member = lax.axis_index("roi")
    partners = [flip(me, 1 << stage) for stage in range(stages)]

    barrier = pltpu.get_barrier_semaphore()
    for partner in partners:
        pl.semaphore_signal(
            barrier, inc=1, device_id=(partner, member), device_id_type=pl.DeviceIdType.MESH
        )
    pl.semaphore_wait(barrier, stages)

    per_array = 1 + 2 * stages - 1 + 5
    parts = []
    for a in range(arrays):
        mine = rest[a * per_array : (a + 1) * per_array]
        own, land, leave = mine[0], mine[1 : 1 + stages], (None,) + mine[1 + stages : 2 * stages]
        parts.append((inputs[a], own, land, leave) + tuple(mine[2 * stages :]))

    def near(a, r):
        source, own, _, _, own_sem, *_ = parts[a]
        slot = r >> 1
        return pltpu.make_async_copy(source.at[flip(me, r)], own.at[slot], own_sem.at[slot])

    def first_copy(a, r):
        source, _, land, _, _, send0, recv0, _, _ = parts[a]
        slot = r >> 1
        return pltpu.make_async_remote_copy(
            src_ref=source.at[flip(me, r)],
            dst_ref=land[0].at[slot],
            send_sem=send0.at[slot],
            recv_sem=recv0.at[slot],
            device_id=(partners[0], member),
            device_id_type=pl.DeviceIdType.MESH,
        )

    def later_copy(a, stage, r, piece):
        _, _, land, leave, _, _, _, send, recv = parts[a]
        rows = piece_rows(land[0].shape[1])
        slot = plan.slot(stage, r)
        at = pl.ds(pl.multiple_of(piece * rows, 16), rows)
        base = sum(plan.count(t) for t in range(1, stage)) + slot
        return pltpu.make_async_remote_copy(
            src_ref=leave[stage].at[slot, at],
            dst_ref=land[stage].at[slot, at],
            send_sem=send.at[base, piece],
            recv_sem=recv.at[base, piece],
            device_id=(partners[stage], member),
            device_id_type=pl.DeviceIdType.MESH,
        )

    for r in plan.order:
        for a in range(arrays):
            first_copy(a, r + 1).start()
        for a in range(arrays):
            near(a, r).start()

    def pieces(a):
        rows = parts[a][2][0].shape[1]
        return rows // piece_rows(rows)

    for r in plan.order:
        stage = lowest_bit(r) if r else stages
        for a in range(arrays):
            _, own, land, leave, *_ = parts[a]
            near(a, r).wait()
            first_copy(a, r).wait_recv()
            rows = piece_rows(land[0].shape[1])

            def step(piece, carry, a=a, own=own, land=land, leave=leave, rows=rows):
                at = pl.ds(pl.multiple_of(piece * rows, 16), rows)
                total = own[r >> 1, at].astype(jnp.float32) + land[0][r >> 1, at].astype(
                    jnp.float32
                )
                for t in range(1, stage):
                    later_copy(a, t, r, piece).wait_recv()
                    total += land[t][plan.slot(t, r), at].astype(jnp.float32)
                if r:
                    leave[stage][plan.slot(stage, r), at] = total.astype(own.dtype)
                    later_copy(a, stage, r, piece).start()
                else:
                    outputs[2 * a][at] = total
                    outputs[2 * a + 1][at] = total.astype(own.dtype)
                return carry

            lax.fori_loop(0, pieces(a), step, 0)

    for r in plan.order:
        for a in range(arrays):
            first_copy(a, r + 1).wait_send()
            if r:
                stage = lowest_bit(r)

                def step(piece, carry, a=a, stage=stage, r=r):
                    later_copy(a, stage, r, piece).wait_send()
                    return carry

                lax.fori_loop(0, pieces(a), step, 0)


def sum_groups(*arrays):
    groups = arrays[0].shape[0]
    plan = SumPlan(groups)
    out_shape, scratch = [], []
    for array in arrays:
        _, rows, width = array.shape
        out_shape += [
            jax.ShapeDtypeStruct((rows, width), jnp.float32),
            jax.ShapeDtypeStruct((rows, width), array.dtype),
        ]
        half = groups // 2
        block = (rows, width)
        scratch += [pltpu.VMEM((half,) + block, array.dtype)]
        scratch += [pltpu.VMEM((plan.count(t),) + block, array.dtype) for t in range(plan.stages)]
        scratch += [
            pltpu.VMEM((plan.count(t),) + block, array.dtype) for t in range(1, plan.stages)
        ]
        later = (half - 1, rows // piece_rows(rows))
        scratch += [pltpu.SemaphoreType.DMA((half,))] * 3
        scratch += [pltpu.SemaphoreType.DMA(later)] * 2
    return pl.pallas_call(
        functools.partial(sum_kernel, plan, len(arrays)),
        in_specs=[pl.BlockSpec(memory_space=pl.ANY)] * len(arrays),
        out_specs=[pl.BlockSpec(memory_space=pltpu.VMEM)] * len(out_shape),
        out_shape=out_shape,
        scratch_shapes=scratch,
        compiler_params=pltpu.CompilerParams(
            collective_id=0, has_side_effects=True, vmem_limit_bytes=56 * MIB
        ),
        name="sum_groups",
    )(*arrays)


def gather_kernel(arrays, plan, *refs):
    inputs, outputs = refs[:arrays], refs[arrays : 2 * arrays]
    own_sem, send, recv = refs[2 * arrays :]
    axes = len(SPLIT)
    sizes = outputs[0].shape[:axes]
    dp = lax.axis_index("dp")
    me = [lax.axis_index("roi")]
    for axis in range(1, axes):
        me.append(dp // math.prod(sizes[axis + 1 :]) % sizes[axis])
    me = tuple(me)

    def device(axis, shift):
        spot = list(me)
        spot[axis] = (me[axis] + shift) % sizes[axis]
        group = spot[1]
        for other in range(2, axes):
            group = group * sizes[other] + spot[other]
        return (group, spot[0])

    barrier = pltpu.get_barrier_semaphore()
    peers = [(axis, shift) for axis in range(axes) for shift in range(1, sizes[axis])]
    for axis, shift in peers:
        pl.semaphore_signal(
            barrier, inc=1, device_id=device(axis, shift), device_id_type=pl.DeviceIdType.MESH
        )
    pl.semaphore_wait(barrier, len(peers))

    def copies(number, stage):
        array, first, rows, order = plan[number]
        done, axis = order[:stage], order[stage]
        held = tuple(slice(None) if d in done else me[d] for d in range(axes))
        at = pl.ds(first, rows)
        region = outputs[array].at[held + (at,)]
        source = inputs[array].at[at] if stage == 0 else region
        before = sum(sizes[d] - 1 for d in done)
        return [
            pltpu.make_async_remote_copy(
                src_ref=source,
                dst_ref=region,
                send_sem=send.at[number, before + shift - 1],
                recv_sem=recv.at[number, before + shift - 1],
                device_id=device(axis, shift),
                device_id_type=pl.DeviceIdType.MESH,
            )
            for shift in range(1, sizes[axis])
        ]

    for number in range(len(plan)):
        for copy in copies(number, 0):
            copy.start()
    own = [
        pltpu.make_async_copy(inputs[a], outputs[a].at[me], own_sem.at[a]) for a in range(arrays)
    ]
    for copy in own:
        copy.start()
    for copy in own:
        copy.wait()
    for stage in range(1, axes + 1):
        for number in range(len(plan)):
            for copy in copies(number, stage - 1):
                copy.wait_recv()
            if stage < axes:
                for copy in copies(number, stage):
                    copy.start()
    for stage in range(axes):
        for number in range(len(plan)):
            for copy in copies(number, stage):
                copy.wait_send()


def gather_all(*arrays):
    members = lax.axis_size("roi")
    groups = lax.axis_size("dp")
    sizes = (members, groups // math.prod(SPLIT[2:])) + SPLIT[2:]
    plan = []
    for a, array in enumerate(arrays):
        rows = array.shape[0]
        step = piece_rows(rows)
        for n, first in enumerate(range(0, rows, step)):
            plan.append((a, first, step, ORDERS[n % len(ORDERS)]))
    copies = sum(size - 1 for size in sizes)
    return pl.pallas_call(
        functools.partial(gather_kernel, len(arrays), plan),
        in_specs=[pl.BlockSpec(memory_space=pl.ANY)] * len(arrays),
        out_specs=[pl.BlockSpec(memory_space=pl.ANY)] * len(arrays),
        out_shape=[jax.ShapeDtypeStruct(sizes + array.shape, array.dtype) for array in arrays],
        scratch_shapes=[
            pltpu.SemaphoreType.DMA((len(arrays),)),
            pltpu.SemaphoreType.DMA((len(plan), copies)),
            pltpu.SemaphoreType.DMA((len(plan), copies)),
        ],
        compiler_params=pltpu.CompilerParams(collective_id=1, has_side_effects=True),
        name="gather_all",
    )(*arrays)


def lane_coordinates(rows, first_lane, lanes):
    cell = lax.broadcasted_iota(jnp.int32, (rows, lanes), 1) + first_lane
    return cell_coordinates(cell)


def cell_coordinates(cell):
    second = cell - FINE
    third = second - FINE // 4
    fourth = third - FINE // 16
    rest = cell - (FINE + FINE // 4 + FINE // 16 + FINE // 64)
    row = jnp.where(
        second < 0,
        cell >> 5,
        jnp.where(
            third < 0,
            second >> 4,
            jnp.where(fourth < 0, (third >> 3) + 32, (fourth >> 2) + 64),
        ),
    )
    column = jnp.where(
        second < 0,
        cell & 31,
        jnp.where(third < 0, second & 15, jnp.where(fourth < 0, third & 7, fourth & 3)),
    )
    row = jnp.where(rest < 0, row, 1000)
    return row.astype(jnp.float32), column.astype(jnp.float32)


def pool_kernel(fine_ref, coarse_ref, place_ref, maps_ref, out_ref, high, low, total):
    tile = pl.program_id(0)
    cells = maps_ref.shape[1]

    def part(first, count, column_of_row, start):
        chunk = 256 if count % 256 == 0 else 128
        for at in range(0, count, chunk):
            row_of, column_of = lane_coordinates(TILE, first + at, chunk)
            across = [hat(place_ref[:, j : j + 1] - column_of) for j in range(POOL)]
            for i in range(POOL):
                spot = column_of_row + i
                down = hat(place_ref[:, spot : spot + 1] - row_of)
                for j in range(POOL):
                    weight = down * across[j]
                    big = weight.astype(jnp.bfloat16)
                    rows = pl.ds((i * POOL + j) * TILE, TILE)
                    high[rows, pl.ds(at, chunk)] = big
                    low[rows, pl.ds(at, chunk)] = (weight - big.astype(jnp.float32)).astype(
                        jnp.bfloat16
                    )
        maps = maps_ref[0, pl.ds(first, count), :]
        product = jnp.dot(high[:, :count], maps, preferred_element_type=jnp.float32)
        product += jnp.dot(low[:, :count], maps, preferred_element_type=jnp.float32)
        if start:
            total[...] = product
        else:
            total[...] += product

    has_fine = fine_ref[tile] > 0
    has_coarse = coarse_ref[tile] > 0

    @pl.when(has_fine)
    def _():
        part(0, FINE, POOL, True)

    @pl.when(jnp.logical_not(has_fine))
    def _():
        total[...] = jnp.zeros_like(total)

    @pl.when(has_coarse)
    def _():
        part(FINE, cells - FINE, 2 * POOL, False)

    channels = maps_ref.shape[2]
    for b in range(BINS):
        out_ref[:, b * channels : (b + 1) * channels] = total[
            b * TILE : (b + 1) * TILE, :
        ].astype(jnp.bfloat16)


def pool(fine, coarse, places, maps, per_image):
    regions = places.shape[0]
    cells, channels = maps.shape[1:]
    tiles = per_image // TILE
    return pl.pallas_call(
        pool_kernel,
        grid_spec=pltpu.PrefetchScalarGridSpec(
            num_scalar_prefetch=2,
            grid=(regions // TILE,),
            in_specs=[
                pl.BlockSpec((TILE, 128), lambda t, *_: (t, 0)),
                pl.BlockSpec((1, cells, channels), lambda t, *_: (t // tiles, 0, 0)),
            ],
            out_specs=pl.BlockSpec((TILE, BINS * channels), lambda t, *_: (t, 0)),
            scratch_shapes=[
                pltpu.VMEM((BINS * TILE, FINE), jnp.bfloat16),
                pltpu.VMEM((BINS * TILE, FINE), jnp.bfloat16),
                pltpu.VMEM((BINS * TILE, channels), jnp.float32),
            ],
        ),
        out_shape=jax.ShapeDtypeStruct((regions, BINS * channels), jnp.bfloat16),
        compiler_params=pltpu.CompilerParams(vmem_limit_bytes=40 * MIB),
        cost_estimate=pl.CostEstimate(
            flops=4 * regions * BINS * 512 * channels,
            bytes_accessed=2 * regions * BINS * channels,
            transcendentals=0,
        ),
        name="pool",
    )(fine, coarse, places, maps)


def unpool_kernel(fine_ref, coarse_ref, place_ref, grad_ref, out_ref, weight, grads, *, tiles):
    tile = pl.program_id(0)
    cells, channels = out_ref.shape[1:]
    lanes = weight.shape[1]

    @pl.when(tile == 0)
    def _():
        grads[BINS * TILE :, :] = jnp.zeros_like(grads[BINS * TILE :, :])

    @pl.when(lax.rem(tile, tiles) == 0)
    def _():
        out_ref[...] = jnp.zeros_like(out_ref)

    for b in range(BINS):
        grads[b * TILE : (b + 1) * TILE, :] = grad_ref[:, b * channels : (b + 1) * channels]
    across = place_ref[0, 0:1, :]

    @pl.when(fine_ref[tile] > 0)
    def _():
        down = place_ref[0, 1:2, :]
        column = lax.broadcasted_iota(jnp.int32, (MAP, lanes), 0).astype(jnp.float32)
        over = hat(across - column)
        for y in range(MAP):
            weight[y * MAP : (y + 1) * MAP, :] = (hat(down - float(y)) * over).astype(jnp.bfloat16)
        out_ref[0, :FINE, :] += jnp.dot(
            weight[:FINE, :], grads[...], preferred_element_type=jnp.float32
        )

    @pl.when(coarse_ref[tile] > 0)
    def _():
        down = place_ref[0, 2:3, :]
        for at in range(FINE, cells, 16):
            cell = lax.broadcasted_iota(jnp.int32, (16, lanes), 0) + at
            row_of, column_of = cell_coordinates(cell)
            weight[at - FINE : at - FINE + 16, :] = (
                hat(down - row_of) * hat(across - column_of)
            ).astype(jnp.bfloat16)
        out_ref[0, FINE:, :] += jnp.dot(
            weight[: cells - FINE, :], grads[...], preferred_element_type=jnp.float32
        )


def unpool(fine, coarse, lane_places, grads, images, cells, channels):
    regions = grads.shape[0]
    count = regions // TILE
    tiles = count // images
    lanes = lane_places.shape[2]
    return pl.pallas_call(
        functools.partial(unpool_kernel, tiles=tiles),
        grid_spec=pltpu.PrefetchScalarGridSpec(
            num_scalar_prefetch=2,
            grid=(count,),
            in_specs=[
                pl.BlockSpec((1, 8, lanes), lambda t, *_: (t, 0, 0)),
                pl.BlockSpec((TILE, BINS * channels), lambda t, *_: (t, 0)),
            ],
            out_specs=pl.BlockSpec((1, cells, channels), lambda t, *_: (t // tiles, 0, 0)),
            scratch_shapes=[
                pltpu.VMEM((FINE, lanes), jnp.bfloat16),
                pltpu.VMEM((lanes, channels), jnp.bfloat16),
            ],
        ),
        out_shape=jax.ShapeDtypeStruct((images, cells, channels), jnp.float32),
        compiler_params=pltpu.CompilerParams(vmem_limit_bytes=40 * MIB),
        cost_estimate=pl.CostEstimate(
            flops=2 * regions * BINS * 512 * channels,
            bytes_accessed=2 * regions * BINS * channels,
            transcendentals=0,
        ),
        name="unpool",
    )(fine, coarse, lane_places, grads)


def split(value):
    high = value.astype(jnp.bfloat16)
    return high, (value - high.astype(jnp.float32)).astype(jnp.bfloat16)


def split_dot(left_side, right_side):
    high, low = split(left_side)
    other_high, other_low = split(right_side)
    product = jnp.dot(high, other_low, preferred_element_type=jnp.float32)
    product += jnp.dot(low, other_high, preferred_element_type=jnp.float32)
    return product + jnp.dot(high, other_high, preferred_element_type=jnp.float32)


def shampoo_kernel(left_ref, root_ref, full_ref, own_ref, right_root_ref, weight_ref,
                   new_left_ref, new_weight_ref, mixed, *, rate):
    step = pl.program_id(0)
    members, _, width = full_ref.shape

    @pl.when(step == 0)
    def _():
        mixed[...] = jnp.zeros_like(mixed)

    root = root_ref[...].astype(jnp.bfloat16)
    gram = rows_by_rows(own_ref[0], full_ref[0])
    for member in range(1, members):
        gram += rows_by_rows(own_ref[member], full_ref[member])
    new_left_ref[...] = BETA * left_ref[...] + (1.0 - BETA) * gram
    for member in range(members):
        mixed[:, member * width : (member + 1) * width] += jnp.dot(
            root, full_ref[member], preferred_element_type=jnp.float32
        )

    @pl.when(step == pl.num_programs(0) - 1)
    def _():
        update = split_dot(mixed[...], right_root_ref[...])
        new_weight_ref[...] = weight_ref[...] - rate * update


def shampoo(left, root, full, own, right_root, weight, rate):
    rows, order = left.shape
    members, _, width = full.shape
    hidden = members * width
    return pl.pallas_call(
        functools.partial(shampoo_kernel, rate=rate),
        grid=(order // COLS,),
        in_specs=[
            pl.BlockSpec((rows, COLS), lambda t: (0, t)),
            pl.BlockSpec((rows, COLS), lambda t: (0, t)),
            pl.BlockSpec((members, COLS, width), lambda t: (0, t, 0)),
            pl.BlockSpec((members, rows, width), lambda t: (0, 0, 0)),
            pl.BlockSpec((hidden, hidden), lambda t: (0, 0)),
            pl.BlockSpec((rows, hidden), lambda t: (0, 0)),
        ],
        out_specs=[
            pl.BlockSpec((rows, COLS), lambda t: (0, t)),
            pl.BlockSpec((rows, hidden), lambda t: (0, 0)),
        ],
        out_shape=[
            jax.ShapeDtypeStruct((rows, order), jnp.float32),
            jax.ShapeDtypeStruct((rows, hidden), jnp.float32),
        ],
        scratch_shapes=[pltpu.VMEM((rows, hidden), jnp.float32)],
        compiler_params=pltpu.CompilerParams(vmem_limit_bytes=48 * MIB),
        cost_estimate=pl.CostEstimate(
            flops=4 * rows * order * hidden,
            bytes_accessed=12 * rows * order + 2 * order * hidden,
            transcendentals=0,
        ),
        name="shampoo",
    )(left, root, full, own, right_root, weight)


def diagonal_step(gradient, weight, moment, step_rate):
    new_moment = DECAY * moment + (1.0 - DECAY) * gradient * gradient
    return (new_moment, weight - step_rate * gradient / (jnp.sqrt(new_moment) + EPSILON))


def local(
    feature_maps,
    region_boxes,
    levels,
    labels,
    image_of_roi,
    targets,
    first_weight,
    second_weight,
    head_weight,
    biases,
    head_moment,
    bias_moment,
    left_first,
    left_first_root,
    right_first,
    right_first_root,
    left_second,
    left_second_root,
    right_second,
    right_second_root,
):
    groups = lax.axis_size("dp")
    members = lax.axis_size("roi")
    dp = lax.axis_index("dp")
    me = lax.axis_index("roi")
    owner = dp * members + me
    region_count = region_boxes.shape[0]
    group_regions = region_count * members
    images, cells, channels = feature_maps.shape
    per_image = group_regions // images
    owned, hidden = first_weight.shape
    width = hidden // members
    owned_second = second_weight.shape[0]
    features = owned * members * groups
    classes = head_weight.shape[1] - 4
    outs = classes + 4
    loss_scale = 1.0 / (region_count * groups * members)

    first_low = first_weight.astype(jnp.bfloat16)
    column_parts = jnp.swapaxes(first_low.reshape(owned, members, width), 0, 1)
    second_block = second_weight.astype(jnp.bfloat16).reshape(owned_second * members, width)
    parts = jnp.concatenate(
        [column_parts, jnp.broadcast_to(second_block, (members,) + second_block.shape)], axis=1
    )
    traded = trade_members(parts)
    payload = jnp.concatenate(
        [
            traded[:, :owned].reshape(members * owned, width),
            traded[:, owned:].reshape(members * members * owned_second, width),
        ],
        axis=0,
    )
    gathered = lax.all_gather(payload, "dp", axis=0)
    right_roots, gathered = lax.optimization_barrier(
        (jnp.stack([right_first_root, right_second_root]), gathered)
    )
    right_roots = lax.all_gather(right_roots, ("dp", "roi"), axis=1, tiled=True)
    first_half = gathered[:, : members * owned].reshape(features, width)
    second_full = gathered[:, members * owned :].reshape(hidden, hidden)

    info = jnp.concatenate(
        [
            region_boxes,
            jnp.stack([levels, image_of_roi - dp * images, labels], axis=1).astype(jnp.float32),
            targets.astype(jnp.float32),
        ],
        axis=1,
    )
    info = gather_members(info).reshape(group_regions, info.shape[1])
    key = info[:, 5] * 4.0 + info[:, 4]
    number = jnp.arange(group_regions, dtype=jnp.int32)
    ahead = (key[None, :] < key[:, None]) | (
        (key[None, :] == key[:, None]) & (number[None, :] < number[:, None])
    )
    position = jnp.sum(ahead.astype(jnp.int32), axis=1)
    chosen = (position[None, :] == number[:, None]).astype(jnp.float32)
    info = jnp.dot(chosen, info, precision=lax.Precision.HIGHEST)
    boxes = info[:, :4]
    level = jnp.round(info[:, 4]).astype(jnp.int32)
    across, down = sample_points(boxes, level)
    fine_down = jnp.where(level[:, None] == 0, down, -64.0)
    coarse_down = jnp.where(
        level[:, None] == 0, -64.0, down + 32.0 * (level[:, None] - 1).astype(jnp.float32)
    )
    count = group_regions // TILE
    fine = jnp.max((level == 0).astype(jnp.int32).reshape(count, TILE), axis=1)
    coarse = jnp.max((level > 0).astype(jnp.int32).reshape(count, TILE), axis=1)
    places = jnp.pad(
        jnp.concatenate([across, fine_down, coarse_down], axis=1), ((0, 0), (0, 128 - 3 * POOL))
    )
    by_tile = places[:, : 3 * POOL].reshape(count, TILE, 3, POOL)
    by_tile = jnp.transpose(by_tile, (0, 2, 3, 1))
    lane_shape = (count, POOL, POOL, TILE)
    lanes = round_up(BINS * TILE, 128)
    lane_places = jnp.stack(
        [
            jnp.broadcast_to(by_tile[:, 0, None, :, :], lane_shape),
            jnp.broadcast_to(by_tile[:, 1, :, None, :], lane_shape),
            jnp.broadcast_to(by_tile[:, 2, :, None, :], lane_shape),
        ],
        axis=1,
    ).reshape(count, 3, BINS * TILE)
    lane_places = jnp.pad(lane_places, ((0, 0), (0, 5), (0, lanes - BINS * TILE)))

    padded_maps = jnp.pad(feature_maps, ((0, 0), (0, round_up(cells, 128) - cells), (0, 0)))
    pooled = pool(fine, coarse, places, padded_maps, per_image)

    head_low = head_weight.astype(jnp.bfloat16)
    bias_first = lax.dynamic_slice_in_dim(biases, me * width, width)
    bias_second = biases[hidden : 2 * hidden]
    bias_head = biases[2 * hidden :]
    first_pre = jnp.dot(pooled, first_half, preferred_element_type=jnp.float32) + bias_first
    first_act = jax.nn.silu(first_pre).astype(jnp.bfloat16)
    act_rows = trade_members(first_act.reshape(members, region_count, width))
    act_rows = jnp.swapaxes(act_rows, 0, 1).reshape(region_count, hidden)
    second_pre = jnp.dot(act_rows, second_full, preferred_element_type=jnp.float32) + bias_second
    second_act = jax.nn.silu(second_pre).astype(jnp.bfloat16)
    head_out = jnp.dot(second_act, head_low, preferred_element_type=jnp.float32) + bias_head
    own_info = lax.dynamic_slice_in_dim(info, me * region_count, region_count, 0)
    own_labels = jnp.round(own_info[:, 6]).astype(jnp.int32)
    logits = head_out[:, :classes]
    deltas = head_out[:, classes:]
    largest = jnp.max(logits, axis=1, keepdims=True)
    shifted = jnp.exp(logits - largest)
    exp_total = jnp.sum(shifted, axis=1, keepdims=True)
    log_total = largest[:, 0] + jnp.log(exp_total[:, 0])
    label_hot = own_labels[:, None] == jnp.arange(classes, dtype=jnp.int32)[None, :]
    picked = jnp.sum(jnp.where(label_hot, logits, 0.0), axis=1)
    foreground = (own_labels > 0).astype(jnp.float32)
    residue = deltas - own_info[:, 7:11] / FIXED_POINT
    loss = log_total - picked + foreground * jnp.sum(huber_loss(residue), axis=1)
    decoded = decode_boxes(own_info[:, :4], deltas)
    results = gather_members(jnp.concatenate([loss[:, None], decoded], axis=1))
    results = results.reshape(group_regions, 5)
    own_position = lax.dynamic_slice_in_dim(position, me * region_count, region_count)
    own_chosen = (own_position[:, None] == number[None, :]).astype(jnp.float32)
    results = jnp.dot(own_chosen, results, precision=lax.Precision.HIGHEST)

    grad_logits = (shifted / exp_total - label_hot.astype(jnp.float32)) * loss_scale
    grad_deltas = foreground[:, None] * jnp.clip(residue, -1.0, 1.0) * loss_scale
    grad_out = jnp.concatenate([grad_logits, grad_deltas], axis=1).astype(jnp.bfloat16)
    head_term = cols_by_cols(second_act, grad_out)
    grad_second_act = rows_by_rows(grad_out, head_low)
    grad_second = (grad_second_act * silu_slope(second_pre)).astype(jnp.bfloat16)
    group_second = gather_members(grad_second).reshape(group_regions, hidden)
    second_rows = lax.dynamic_slice_in_dim(second_full, me * width, width, 0)
    grad_first = (rows_by_rows(group_second, second_rows) * silu_slope(first_pre)).astype(
        jnp.bfloat16
    )
    first_term = cols_by_cols(pooled, grad_first).astype(jnp.bfloat16)
    second_term = cols_by_cols(first_act, group_second).astype(jnp.bfloat16)
    block = features // groups
    padding = round_up(block, 16) - block
    first_term = first_term.reshape(groups, block, width)
    if padding:
        first_term = jnp.pad(first_term, ((0, 0), (0, padding), (0, 0)))
    second_term = second_term.reshape(groups, -1, width)
    zeros = jnp.zeros((hidden,), jnp.float32)
    bias_term = jnp.concatenate(
        [
            lax.dynamic_update_slice_in_dim(
                zeros, jnp.sum(grad_first, axis=0, dtype=jnp.float32), me * width, 0
            ),
            jnp.sum(grad_second, axis=0, dtype=jnp.float32),
            jnp.sum(grad_out, axis=0, dtype=jnp.float32),
        ]
    )
    small_rows = round_up(hidden + (biases.shape[0] + 127) // 128, 16 * groups)
    bias_space = (small_rows - hidden) * 128
    small_term = jnp.concatenate(
        [
            jnp.pad(head_term, ((0, 0), (0, 128 - outs))),
            jnp.pad(bias_term, (0, bias_space - bias_term.shape[0])).reshape(-1, 128),
        ],
        axis=0,
    ).reshape(groups, small_rows // groups, 128)
    first_sum, first_sum_low, second_sum, second_sum_low, small_sum, _ = sum_groups(
        first_term, second_term, small_term
    )

    grad_pooled = rows_by_rows(grad_first, first_half).astype(jnp.bfloat16)
    map_partial = unpool(fine, coarse, lane_places, grad_pooled, images, cells, channels)
    map_parts = map_partial.reshape(images, members, cells // members, channels)
    map_parts = jnp.swapaxes(map_parts, 0, 1)
    map_own = lax.dynamic_index_in_dim(map_parts, me, 0, keepdims=False)
    map_traded = trade_members(map_parts.astype(jnp.bfloat16)).astype(jnp.float32)
    keep = (jnp.arange(members) == me)[:, None, None, None]
    map_gradient = map_own + jnp.sum(jnp.where(keep, 0.0, map_traded), axis=0)

    first_gradient = trade_members(first_sum[:block].reshape(members, owned, width))
    first_gradient = jnp.swapaxes(first_gradient, 0, 1).reshape(owned, hidden)
    devices = groups * members
    second_gradient = lax.ppermute(
        second_sum.reshape(owned_second, hidden),
        ("dp", "roi"),
        [((b % groups) * members + b // groups, b) for b in range(devices)],
    )
    first_reduced, second_reduced, small = gather_all(first_sum_low, second_sum_low, small_sum)
    small = jnp.sum(small.reshape(members, small_rows, 128), axis=0)
    head_gradient = small[:hidden, :outs]
    bias_gradient = small[hidden:].reshape(-1)[: biases.shape[0]]
    first_reduced = first_reduced.reshape(members, groups, block + padding, width)
    first_reduced = first_reduced[:, :, :block].reshape(members, features, width)
    second_reduced = second_reduced.reshape(hidden, hidden)
    own_first = lax.dynamic_slice_in_dim(first_reduced, owner * owned, owned, 1)
    new_left_first, new_first_weight = shampoo(
        left_first, left_first_root, first_reduced, own_first, right_roots[0], first_weight,
        RATE_FIRST,
    )
    own_rows = right_first.shape[0]
    which = owner * own_rows // width
    own_columns = lax.dynamic_slice(
        first_reduced, (which, 0, owner * own_rows - which * width), (1, features, own_rows)
    )[0]
    first_gram = jnp.concatenate(
        [cols_by_cols(own_columns, first_reduced[member]) for member in range(members)], axis=1
    )
    new_right_first = BETA * right_first + (1.0 - BETA) * first_gram

    own_second = lax.dynamic_slice_in_dim(second_reduced, owner * owned_second, owned_second, 0)
    own_columns = lax.dynamic_slice_in_dim(second_reduced, owner * own_rows, own_rows, 1)
    new_left_second = BETA * left_second + (1.0 - BETA) * rows_by_rows(own_second, second_reduced)
    new_right_second = BETA * right_second + (1.0 - BETA) * cols_by_cols(
        own_columns, second_reduced
    )
    mixed = jnp.dot(
        left_second_root.astype(jnp.bfloat16), second_reduced, preferred_element_type=jnp.float32
    )
    update = split_dot(mixed, right_roots[1])
    new_second_weight = second_weight - RATE_SECOND * update

    new_head_moment, new_head_weight = diagonal_step(
        head_gradient, head_weight, head_moment, RATE_HEAD
    )
    new_bias_moment, new_biases = diagonal_step(bias_gradient, biases, bias_moment, RATE_BIAS)
    return (
        results[:, 0],
        results[:, 1:],
        map_gradient,
        first_gradient,
        new_left_first,
        new_right_first,
        new_first_weight,
        second_gradient,
        new_left_second,
        new_right_second,
        new_second_weight,
        head_gradient,
        new_head_moment,
        new_head_weight,
        bias_gradient,
        new_bias_moment,
        new_biases,
    )


def solution(mesh):
    rows = P(("dp", "roi"), None)
    flat = P(("dp", "roi"))
    return jax.shard_map(
        local,
        mesh=mesh,
        in_specs=(P("dp", None, None), rows, flat, flat, flat, rows, rows, rows)
        + (P(),) * 4
        + (rows,) * 8,
        out_specs=(flat, rows, P("dp", "roi", None)) + (rows,) * 8 + (P(),) * 6,
        check_vma=False,
    )
```
